512 devices in a mesh: segment: 2 (over x_hi), lat: 8 (over y, core), lon: 32 (over x_lo, z).
Axes of the slice: x: 4 (x_hi: 2, x_lo: 2; x = x_hi * 2 + x_lo), y: 4, z: 16, core: 2. Of those that a mesh axis runs over, the one named last changes fastest.
Arguments:
- inputs: bfloat16 [2, 16, 1440, 256], P(None, 'lat', 'lon'), may hold values from -6 to 6
- cotangent: bfloat16 [2, 16, 1440, 256], P(None, 'lat', 'lon'), may hold values from -6 to 6
- weights: bfloat16 [2, 2304, 256], P('segment'), may hold values from -0.125 to 0.125
- psi: bfloat16 [9, 16, 3, 17], replicated, may hold values from -1.25 to 1.25
- band_half: int32 [16, 3], replicated, may hold values from 1 to 8, as said below
Outputs:
- sections: bfloat16 [2, 2, 16, 1440, 256], P('segment', None, 'lat', 'lon')
- weight_grads: float32 [2, 2304, 256], P('segment')
The draws below stay inside these ranges and needn't reach their ends.
Inputs may be any that keep to these rules, and one draw needn't show every extreme that they name: `band_half`: rows 0 and 15 have the half-width 8 at every offset.
All inputs are finite; a program needn't handle non-finite values.
Results may differ from the reference program's by a relative error of at most 0.0076.
Values may be sent and summed in bfloat16 or wider, within the bound.
No kernel may reach another device: no remote copies, remote signals or barrier semaphores. Data moves between devices by JAX's collectives and lax.ppermute only.
A program may use at most 64 MiB of HBM per device.

```python
import jax
import jax.numpy as jnp
from jax import lax

C = 256
K = 9
H = 8
MB = 2
LOND = 45
BW = 17
NLAT = 16
NLON = 1440


def draw_band_half(key, part):
    key = jax.random.fold_in(key, 7)
    halves = jax.random.randint(key, (NLAT, 3), 1, H + 1)
    rows = jnp.arange(NLAT)[:, None] + jnp.zeros((1, 3), jnp.int32)
    polar = (rows == 0) | (rows == NLAT - 1)
    return jnp.where(polar, H, halves).astype(jnp.int32)


def shard_levels(key, shape, shards, low, high):
    def one(position, blocks):
        steps = jax.random.uniform(jax.random.fold_in(jax.random.fold_in(key, 6), position), (blocks,), jnp.float32, low / len(shards), high / len(shards))
        return jnp.repeat(jnp.exp(steps), shape[position] // blocks).reshape((-1,) + (1,) * (len(shape) - position - 1))

    level = one(*shards[0])
    for cut in shards[1:]:
        level = level * one(*cut)
    return level


def scatter_about(own_key, extent, deviation, most, pieces=(), held_as=jnp.bfloat16):
    factor_of = shard_levels(own_key, extent, pieces, -0.22, 0.18) if pieces else 1.0
    array = jax.random.normal(own_key, extent, jnp.float32) * deviation * factor_of
    return jnp.minimum(jnp.maximum(array, -most), most).astype(held_as)


def setup_inputs(seed: int = 0) -> dict:
    arg_keys = jax.random.split(jax.random.key(seed), 6)
    inputs = scatter_about(arg_keys[0], (MB, NLAT, NLON, C), 1.0, 6.0, ((1, 8), (2, 32)))
    cotangent = scatter_about(arg_keys[1], (MB, NLAT, NLON, C), 1.0, 6.0, ((1, 8), (2, 32)))
    weights = scatter_about(arg_keys[2], (2, K * C, C), (K * C) ** -0.5, 0.125, ((0, 2),))
    psi = scatter_about(arg_keys[3], (K, NLAT, 3, BW), (3 * BW // 2) ** -0.5, 1.25)
    band_half = draw_band_half(jax.random.fold_in(arg_keys[5], 71), 0)
    return dict(inputs=inputs, cotangent=cotangent, weights=weights, psi=psi, band_half=band_half)


def tap_table():
    outer = lax.broadcasted_iota(jnp.int32, (LOND, LOND + 2 * H, BW), 0)
    inner = lax.broadcasted_iota(jnp.int32, (LOND, LOND + 2 * H, BW), 1)
    tapped = lax.broadcasted_iota(jnp.int32, (LOND, LOND + 2 * H, BW), 2)
    return (inner - outer == tapped).astype(jnp.float32)

def banded(field, toeplitz):
    padded = jnp.pad(field, ((0, 0), (1, 1), (0, 0), (0, 0)))
    padded = jnp.concatenate([padded[:, :, NLON - H:], padded, padded[:, :, :H]], axis=2)
    block_index = jnp.arange(NLON // LOND, dtype=jnp.int32)[:, None] * LOND + jnp.arange(LOND + 2 * H, dtype=jnp.int32)[None, :]

    def one_row(row_index):
        slab = lax.dynamic_slice_in_dim(padded, row_index, 3, 1)
        blocks = slab[:, :, block_index]
        table = lax.dynamic_index_in_dim(toeplitz, row_index, 1, keepdims=False)
        result = jnp.einsum('kaoj,manjc->mnokc', table, blocks, precision=lax.Precision.HIGHEST)
        return result.reshape(MB, NLON, K * field.shape[3])
    stacked = lax.map(one_row, jnp.arange(NLAT, dtype=jnp.int32))
    return jnp.transpose(stacked, (1, 0, 2, 3))

def gelu_back(preact, incoming):
    return jax.vjp(jax.nn.gelu, preact)[1](incoming)[0]

def reference(inputs, cotangent, weights, psi, band_half):
    taps = lax.broadcasted_iota(jnp.int32, psi.shape, 3)
    live = jnp.abs(taps - H) <= band_half[None, :, :, None]
    effective = jnp.where(live, psi, jnp.zeros_like(psi)).astype(jnp.float32)
    toeplitz = jnp.einsum('krab,ojb->kraoj', effective, tap_table(), precision=lax.Precision.HIGHEST)

    def layer(field, matrix):
        basis = banded(field.astype(jnp.float32), toeplitz).astype(jnp.bfloat16)
        preact = jnp.einsum('mrjq,qc->mrjc', basis.astype(jnp.float32), matrix.astype(jnp.float32), precision=lax.Precision.HIGHEST)
        result = (field.astype(jnp.float32) + jax.nn.gelu(preact)).astype(jnp.bfloat16)
        return (result, basis, preact)
    output_first, basis_first, preact_first = layer(inputs, weights[0])
    output_second, basis_second, preact_second = layer(output_first, weights[1])
    units_second = gelu_back(preact_second, cotangent.astype(jnp.float32)).astype(jnp.bfloat16)
    mixed = jnp.einsum('mrjd,qd->mrjq', units_second.astype(jnp.float32), weights[1].astype(jnp.float32), precision=lax.Precision.HIGHEST)
    pullback = jax.vjp(lambda field: banded(field, toeplitz), jnp.zeros((MB, NLAT, NLON, C), jnp.float32))[1]
    back_band = pullback(mixed)[0]
    grad_first = (cotangent.astype(jnp.float32) + back_band).astype(jnp.bfloat16)
    units_first = gelu_back(preact_first, grad_first.astype(jnp.float32)).astype(jnp.bfloat16)
    grad_w_first = jnp.dot(basis_first.reshape(-1, K * C).T, units_first.reshape(-1, C), preferred_element_type=jnp.float32)
    grad_w_second = jnp.dot(basis_second.reshape(-1, K * C).T, units_second.reshape(-1, C), preferred_element_type=jnp.float32)
    sections = jnp.stack([output_first, output_second])
    return (sections, jnp.stack([grad_w_first, grad_w_second]))
```

```python
import jax
import jax.numpy as jnp
from jax import lax
from jax.sharding import PartitionSpec as P


def with_halo(cells, sides, width, closed):
    for axis, dim in sides:
        count = lax.axis_size(axis)
        ends = count if closed else count - 1
        head = lax.slice_in_dim(cells, 0, width, axis=dim)
        tail = lax.slice_in_dim(cells, cells.shape[dim] - width, cells.shape[dim], axis=dim)
        cells = jnp.concatenate(
            [
                lax.ppermute(tail, axis, [(i, (i + 1) % count) for i in range(ends)]),
                cells,
                lax.ppermute(head, axis, [((i + 1) % count, i) for i in range(ends)]),
            ],
            axis=dim,
        )
    return cells


def shifted(block, axis, distance):
    devices = range(lax.axis_size(axis))
    route = [(i - distance, i) for i in devices if i - distance in devices]
    return lax.ppermute(block, axis, route)


def tap_table(lond, width, flipped):
    shape = (lond, lond + width - 1, width)
    outer = lax.broadcasted_iota(jnp.int32, shape, 0)
    inner = lax.broadcasted_iota(jnp.int32, shape, 1)
    tapped = lax.broadcasted_iota(jnp.int32, shape, 2)
    if flipped:
        tapped = width - 1 - tapped
    return (inner - outer == tapped).astype(jnp.bfloat16)


def gelu_back(preact, incoming):
    return jax.vjp(jax.nn.gelu, preact)[1](incoming)[0]


def neighbours_summed(grads):
    lats, lons = lax.axis_size("lat"), lax.axis_size("lon")
    rows, chans = grads.shape
    half = rows // 2
    depth = 16
    planes = lons // depth
    columns = lats // 2 * planes
    swap = [(i, i ^ 1) for i in range(lats)]
    near = [
        [(2 * y + core) * lons + x * depth + z for y in range(lats // 2) for x in range(planes)]
        for core in range(2)
        for z in range(depth)
    ]
    far = [[x * depth + z for z in range(depth)] for x in range(planes)]
    core = lax.axis_index("lat") % 2
    halves = grads.reshape(2, half, chans)
    keep = lax.dynamic_index_in_dim(halves, core, 0, keepdims=False)
    give = lax.dynamic_index_in_dim(halves, 1 - core, 0, keepdims=False).astype(jnp.bfloat16)
    own = (keep + lax.ppermute(give, "lat", swap).astype(jnp.float32)).astype(jnp.bfloat16)
    own = own.reshape(columns, half // columns, chans)
    own = lax.all_to_all(own, ("lat", "lon"), 0, 0, axis_index_groups=near)
    own = jnp.sum(own.astype(jnp.float32), axis=0).astype(jnp.bfloat16)
    own = own.reshape(depth, half // columns // depth, chans)
    own = lax.all_to_all(own, "lon", 0, 0, axis_index_groups=far)
    own = jnp.sum(own.astype(jnp.float32), axis=0).astype(jnp.bfloat16)
    own = jnp.broadcast_to(own[None], (depth,) + own.shape)
    own = lax.all_to_all(own, "lon", 0, 0, axis_index_groups=far).reshape(-1, chans)
    own = jnp.broadcast_to(own[None], (columns,) + own.shape)
    own = lax.all_to_all(own, ("lat", "lon"), 0, 0, axis_index_groups=near).reshape(-1, chans)
    other = lax.ppermute(own, "lat", swap)
    first = jnp.where(core == 0, own, other)
    second = jnp.where(core == 0, other, own)
    return jnp.concatenate([first, second], axis=0).astype(jnp.float32)


def shards(inputs, cotangent, weights, psi, band_half):
    micro, latd, lond, chans = inputs.shape
    kernels = psi.shape[0]
    width = psi.shape[3]
    reach = (width - 1) // 2
    segment_first = lax.axis_index("segment") == 0
    lat_start = lax.axis_index("lat") * latd
    taps = lax.broadcasted_iota(jnp.int32, psi.shape, 3)
    live = jnp.abs(taps - reach) <= band_half[None, :, :, None]
    effective = jnp.where(live, psi, jnp.zeros_like(psi))
    padded = jnp.pad(effective, ((0, 0), (1, 1), (0, 0), (0, 0)))
    forward_rows = lax.dynamic_slice_in_dim(padded, lat_start + 1, latd, 1)
    toeplitz = jnp.einsum(
        "krab,ojb->kraoj",
        forward_rows,
        tap_table(lond, width, False),
        preferred_element_type=jnp.float32,
    ).astype(jnp.bfloat16)
    adjoint = jnp.stack(
        [
            jnp.einsum(
                "kib,ojb->kioj",
                lax.dynamic_slice_in_dim(padded[:, :, offset], lat_start + 2 - offset, latd, 1),
                tap_table(lond, width, True),
                preferred_element_type=jnp.float32,
            )
            for offset in range(3)
        ],
        axis=2,
    ).astype(jnp.bfloat16)
    matrix = weights[0]

    def extend(field):
        rowwise = with_halo(field, (("lat", 1),), 1, False)
        return with_halo(rowwise, (("lon", 2),), reach, True)

    def forward_windows(extended):
        return jnp.stack([extended[:, offset : offset + latd] for offset in range(3)], axis=2)

    def layer(field):
        windows = forward_windows(extend(field))
        count = field.shape[0]
        raw = jnp.einsum(
            "kiaoj,miajc->ikomc", toeplitz, windows, preferred_element_type=jnp.float32
        )
        basis = jnp.transpose(raw.astype(jnp.bfloat16), (3, 0, 2, 1, 4))
        basis = basis.reshape(count, latd, lond, kernels * chans)
        preact = jnp.einsum("mioq,qc->mioc", basis, matrix, preferred_element_type=jnp.float32)
        result = (field.astype(jnp.float32) + jax.nn.gelu(preact)).astype(jnp.bfloat16)
        return (result, basis, preact)

    out_early, basis_early, preact_early = layer(inputs)
    carried = shifted(out_early, "segment", 1)
    out_late, basis_late, preact_late = layer(carried)
    own_output = jnp.where(segment_first, out_early, out_late)
    own_basis = jnp.where(segment_first, basis_early, basis_late)
    own_preact = jnp.where(segment_first, preact_early, preact_late)
    units_last = gelu_back(own_preact, cotangent.astype(jnp.float32)).astype(jnp.bfloat16)
    mixed = jnp.einsum("miod,qd->mioq", units_last, matrix, preferred_element_type=jnp.float32)
    rowwise = with_halo(mixed.astype(jnp.bfloat16), (("lat", 1),), 1, False).astype(mixed.dtype)
    extended = with_halo(rowwise.astype(jnp.bfloat16), (("lon", 2),), reach, True).astype(
        rowwise.dtype
    )
    spread = extended.reshape(micro, latd + 2, lond + 2 * reach, kernels, chans)
    folded = jnp.einsum(
        "kiaoj,miajkc->iomc",
        adjoint.astype(jnp.float32),
        jnp.stack([spread[:, 2 - offset : 2 - offset + latd] for offset in range(3)], axis=2),
        precision=lax.Precision.HIGHEST,
    )
    back_band = jnp.transpose(folded, (2, 0, 1, 3))
    grad_first = (cotangent.astype(jnp.float32) + back_band).astype(jnp.bfloat16)
    returned = shifted(grad_first, "segment", -1)
    own_grad = jnp.where(segment_first, returned, cotangent)
    own_units = gelu_back(own_preact, own_grad.astype(jnp.float32)).astype(jnp.bfloat16)
    local_grads = lax.dot_general(
        own_basis.reshape(-1, kernels * chans),
        own_units.reshape(-1, chans),
        (((0,), (0,)), ((), ())),
        preferred_element_type=jnp.float32,
    )
    total_grads = neighbours_summed(local_grads)
    return (own_output[None], total_grads[None])


def solution(mesh):
    placed = (
        P(None, "lat", "lon", None),
        P(None, "lat", "lon", None),
        P("segment", None, None),
        P(),
        P(),
    )
    return jax.shard_map(
        shards,
        mesh=mesh,
        in_specs=placed,
        out_specs=(P("segment", None, "lat", "lon", None), P("segment", None, None)),
        check_vma=False,
    )
```

```python
import functools

import jax
import jax.numpy as jnp
from jax import lax
from jax.experimental import pallas as pl
from jax.experimental.pallas import tpu as pltpu
from jax.sharding import PartitionSpec as P

EDGE = 24
LANES = 128
SPAN = 96
CURVE = 0.7978845608028654
CUBIC = 0.044715


def routed(block, axis, distance, closed):
    count = lax.axis_size(axis)
    if closed:
        route = [(i, (i + distance) % count) for i in range(count)]
    else:
        route = [(i, i + distance) for i in range(count) if 0 <= i + distance < count]
    return lax.ppermute(block, axis, route)


def gelu_slope(x):
    squared = x * x
    bend = jnp.tanh(CURVE * (x + CUBIC * x * squared))
    inner = CURVE * (1.0 + 3.0 * CUBIC * squared)
    return 0.5 * (1.0 + bend) + 0.5 * x * (1.0 - bend * bend) * inner


def device_kernel(
    flags,
    taps,
    field,
    own_matrix,
    other_near,
    other_far,
    section,
    keep,
    give,
    table,
    matrices,
    basis0,
    basis1,
    middle,
    preact0,
    units1,
    spread,
    chosen_basis,
    chosen_units,
    grads,
):
    f32, bf16 = jnp.float32, jnp.bfloat16
    kernels = 9
    rows, chans = own_matrix.shape
    half = rows // 2
    reach = 8
    segment, core = flags[0], flags[1]
    window = kernels * SPAN
    lond = section.shape[2]
    near_start = pl.multiple_of(core * half, half)
    far_start = pl.multiple_of((1 - core) * half, half)

    def build(i, carry):
        for a in range(3):
            lanes = slice(a * LANES, (a + 1) * LANES)
            row = jnp.broadcast_to(taps[i, :, lanes], (SPAN, LANES))
            table[i, :, lanes] = pltpu.roll(
                row, LANES - reach, 1, stride=1, stride_axis=0
            ).astype(bf16)
        return carry

    lax.fori_loop(0, 6 * kernels, build, 0)

    matrices[segment] = own_matrix[...]
    matrices[1 - segment, pl.ds(near_start, half)] = other_near[...]
    matrices[1 - segment, pl.ds(far_start, half)] = other_far[...]

    def convolve(i, lines, skip, source, basis):
        m, r = lax.div(i, lines), lax.rem(i, lines)
        slab = source[m, pl.ds(r, 3)].reshape(3 * LANES, chans)
        rows_of = table[pl.ds((r + skip) * kernels, kernels)].reshape(window, 3 * LANES)
        out = jnp.dot(rows_of, slab, preferred_element_type=f32)
        start = pl.multiple_of(i * SPAN, SPAN)
        for k in range(kernels):
            basis[pl.ds(start, SPAN), k * chans : (k + 1) * chans] = out[
                k * SPAN : (k + 1) * SPAN
            ].astype(bf16)

    def first_basis(i, carry):
        convolve(i, 6, 0, field, basis0)
        return carry

    lax.fori_loop(0, 12, first_basis, 0)

    def first_mix(m, carry):
        start = pl.multiple_of(m * 6 * SPAN, 6 * SPAN)
        pre = jnp.dot(
            basis0[pl.ds(start, 6 * SPAN), :], matrices[0], preferred_element_type=f32
        )
        centre = field[m, 1:7, :SPAN].astype(f32).reshape(6 * SPAN, chans)
        out = centre + jax.nn.gelu(pre)
        middle[m, :, :SPAN] = out.astype(bf16).reshape(6, SPAN, chans)
        middle[m, :, SPAN:] = jnp.zeros((6, LANES - SPAN, chans), bf16)
        preact0[m] = pre[2 * SPAN : 4 * SPAN].reshape(2, SPAN, chans)
        return carry

    lax.fori_loop(0, 2, first_mix, 0)

    def second_basis(i, carry):
        convolve(i, 4, 1, middle, basis1)
        return carry

    lax.fori_loop(0, 8, second_basis, 0)

    def second_mix(m, carry):
        start = pl.multiple_of(m * 4 * SPAN, 4 * SPAN)
        pre = jnp.dot(
            basis1[pl.ds(start, 4 * SPAN), :], matrices[1], preferred_element_type=f32
        )
        incoming = field[m, 8:12, :SPAN].astype(f32).reshape(4 * SPAN, chans)
        units1[pl.ds(start, 4 * SPAN), :] = (incoming * gelu_slope(pre)).astype(bf16)
        for p in range(2):
            own = middle[m, p + 2, :SPAN].astype(f32)
            late = own + jax.nn.gelu(pre[(p + 1) * SPAN : (p + 2) * SPAN])
            picked = jnp.where(segment == 0, own, late)
            section[m, p] = picked[EDGE : EDGE + lond].astype(bf16)
        return carry

    lax.fori_loop(0, 2, second_mix, 0)

    column = lax.broadcasted_iota(jnp.int32, (SPAN, chans), 0)
    live = (column >= EDGE) & (column < EDGE + lond)

    @pl.when(segment == 0)
    def _():
        def unmix(k, carry):
            depth = pl.multiple_of(k * chans, chans)
            place = pl.multiple_of(k * SPAN, SPAN)
            mixed = lax.dot_general(
                units1[...],
                matrices[1, pl.ds(depth, chans), :],
                (((1,), (1,)), ((), ())),
                preferred_element_type=f32,
            ).astype(bf16)
            for m in range(2):
                for s in range(4):
                    begin = (m * 4 + s) * SPAN
                    spread[s, pl.ds(place, SPAN), m * chans : (m + 1) * chans] = mixed[
                        begin : begin + SPAN
                    ]
            return carry

        lax.fori_loop(0, kernels, unmix, 0)
        for p in range(2):
            back = jnp.zeros((LANES, 2 * chans), f32)
            for a in range(3):
                s = p + 2 - a
                rows_of = table[
                    (s + 1) * kernels : (s + 2) * kernels, :, a * LANES : (a + 1) * LANES
                ].reshape(window, LANES)
                back += lax.dot_general(
                    rows_of,
                    spread[s],
                    (((0,), (0,)), ((), ())),
                    preferred_element_type=f32,
                )
            for m in range(2):
                place = (m * 2 + p) * SPAN
                total = field[m, 9 + p, :SPAN].astype(f32) + back[
                    :SPAN, m * chans : (m + 1) * chans
                ]
                grad = total.astype(bf16).astype(f32)
                unit = grad * gelu_slope(preact0[m, p])
                chosen_units[place : place + SPAN, :] = jnp.where(live, unit, 0.0).astype(bf16)
                begin = (m * 6 + p + 2) * SPAN
                chosen_basis[place : place + SPAN, :] = basis0[begin : begin + SPAN, :]

    @pl.when(segment != 0)
    def _():
        for p in range(2):
            for m in range(2):
                place = (m * 2 + p) * SPAN
                begin = (m * 4 + p + 1) * SPAN
                unit = units1[begin : begin + SPAN, :].astype(f32)
                chosen_units[place : place + SPAN, :] = jnp.where(live, unit, 0.0).astype(bf16)
                chosen_basis[place : place + SPAN, :] = basis1[begin : begin + SPAN, :]

    for k in range(kernels):
        grads[k * chans : (k + 1) * chans, :] = lax.dot_general(
            chosen_basis[:, k * chans : (k + 1) * chans],
            chosen_units[...],
            (((0,), (0,)), ((), ())),
            preferred_element_type=f32,
        )
    keep[...] = grads[pl.ds(near_start, half), :]
    give[...] = grads[pl.ds(far_start, half), :].astype(bf16)


def on_device(flags, taps, field, own_matrix, other_near, other_far, lond):
    rows, chans = own_matrix.shape
    half = rows // 2
    bf16, f32 = jnp.bfloat16, jnp.float32
    whole = pl.BlockSpec(memory_space=pltpu.VMEM)
    return pl.pallas_call(
        device_kernel,
        out_shape=(
            jax.ShapeDtypeStruct((2, 2, lond, chans), bf16),
            jax.ShapeDtypeStruct((half, chans), f32),
            jax.ShapeDtypeStruct((half, chans), bf16),
        ),
        in_specs=[pl.BlockSpec(memory_space=pltpu.SMEM)] + [whole] * 5,
        out_specs=(whole, whole, whole),
        scratch_shapes=[
            pltpu.VMEM((54, SPAN, 3 * LANES), bf16),
            pltpu.VMEM((2, rows, chans), bf16),
            pltpu.VMEM((12 * SPAN, rows), bf16),
            pltpu.VMEM((8 * SPAN, rows), bf16),
            pltpu.VMEM((2, 6, LANES, chans), bf16),
            pltpu.VMEM((2, 2, SPAN, chans), f32),
            pltpu.VMEM((8 * SPAN, chans), bf16),
            pltpu.VMEM((4, 9 * SPAN, 2 * chans), bf16),
            pltpu.VMEM((4 * SPAN, rows), bf16),
            pltpu.VMEM((4 * SPAN, chans), bf16),
            pltpu.VMEM((rows, chans), f32),
        ],
        compiler_params=pltpu.CompilerParams(vmem_limit_bytes=52 * 1024 * 1024),
        name="sphere",
    )(flags, taps, field, own_matrix, other_near, other_far)


def gathered_sum(keep, give):
    lats, lons = lax.axis_size("lat"), lax.axis_size("lon")
    half, chans = keep.shape
    depth = 16
    planes = lons // depth
    columns = lats // 2 * planes
    swap = [(i, i ^ 1) for i in range(lats)]
    near = [
        [(2 * y + core) * lons + x * depth + z for y in range(lats // 2) for x in range(planes)]
        for core in range(2)
        for z in range(depth)
    ]
    far = [[x * depth + z for z in range(depth)] for x in range(planes)]
    core = lax.axis_index("lat") % 2
    own = (keep + lax.ppermute(give, "lat", swap).astype(jnp.float32)).astype(jnp.bfloat16)
    own = own.reshape(columns, half // columns, chans)
    own = lax.all_to_all(own, ("lat", "lon"), 0, 0, axis_index_groups=near)
    own = jnp.sum(own.astype(jnp.float32), axis=0).astype(jnp.bfloat16)
    own = own.reshape(depth, half // columns // depth, chans)
    own = lax.all_to_all(own, "lon", 0, 0, axis_index_groups=far)
    own = jnp.sum(own.astype(jnp.float32), axis=0).astype(jnp.bfloat16)
    own = jnp.broadcast_to(own[None], (depth,) + own.shape)
    own = lax.all_to_all(own, "lon", 0, 0, axis_index_groups=far).reshape(-1, chans)
    own = jnp.broadcast_to(own[None], (columns,) + own.shape)
    own = lax.all_to_all(own, ("lat", "lon"), 0, 0, axis_index_groups=near).reshape(-1, chans)
    other = lax.ppermute(own, "lat", swap)
    first = jnp.where(core == 0, own, other)
    second = jnp.where(core == 0, other, own)
    return jnp.concatenate([first, second], axis=0).astype(jnp.float32)


def tap_rows(psi, band_half, lat_start):
    kernels, lines, offsets, width = psi.shape
    taps = lax.broadcasted_iota(jnp.int32, psi.shape, 3)
    live = jnp.abs(taps - (width - 1) // 2) <= band_half[None, :, :, None]
    effective = jnp.where(live, psi, jnp.zeros_like(psi)).astype(jnp.float32)
    by_row = jnp.transpose(effective, (1, 0, 2, 3))
    by_row = jnp.pad(by_row, ((2, 2), (0, 0), (0, 0), (0, LANES - width)))
    own = lax.dynamic_slice_in_dim(by_row, lat_start, 6, 0)
    return own.reshape(6 * kernels, 1, offsets * LANES)


def widened(inputs, cotangent):
    lond = inputs.shape[2]
    both = jnp.concatenate([inputs, cotangent[:, 1:]], axis=1)
    down = routed(both, "lat", 1, False)
    both = jnp.concatenate([inputs, cotangent[:, :1]], axis=1)
    up = routed(both, "lat", -1, False)
    down_far = routed(inputs[:, 1:], "lat", 2, False)
    up_far = routed(inputs[:, :1], "lat", -2, False)
    lines = jnp.concatenate(
        [
            down_far,
            down[:, :2],
            inputs,
            up[:, :2],
            up_far,
            down[:, 2:],
            cotangent,
            up[:, 2:],
        ],
        axis=1,
    )
    left = routed(lines[:, :, lond - EDGE :], "lon", 1, True)
    right = routed(lines[:, :, :EDGE], "lon", -1, True)
    blank = jnp.zeros(lines.shape[:2] + (LANES - lond - 2 * EDGE, lines.shape[3]), lines.dtype)
    return jnp.concatenate([left, lines, right, blank], axis=2)


def shards(inputs, cotangent, weights, psi, band_half):
    lat = lax.axis_index("lat")
    core = lat % 2
    segment = lax.axis_index("segment")
    matrix = weights[0]
    half = matrix.shape[0] // 2
    mine = lax.dynamic_slice_in_dim(matrix, core * half, half, 0)
    other_near = lax.ppermute(mine, "segment", [(0, 1), (1, 0)])
    field = widened(inputs, cotangent)
    other_far = lax.ppermute(
        other_near, "lat", [(i, i ^ 1) for i in range(lax.axis_size("lat"))]
    )
    taps = tap_rows(psi, band_half, lat * inputs.shape[1])
    flags = jnp.stack([segment, core]).astype(jnp.int32)
    section, keep, give = on_device(
        flags, taps, field, matrix, other_near, other_far, inputs.shape[2]
    )
    return (section[None], gathered_sum(keep, give)[None])


def solution(mesh):
    placed = (
        P(None, "lat", "lon", None),
        P(None, "lat", "lon", None),
        P("segment", None, None),
        P(),
        P(),
    )
    return jax.shard_map(
        shards,
        mesh=mesh,
        in_specs=placed,
        out_specs=(P("segment", None, "lat", "lon", None), P("segment", None, None)),
        check_vma=False,
    )
```

```python
import functools

import jax
import jax.numpy as jnp
from jax import lax
from jax.experimental import pallas as pl
from jax.experimental.pallas import tpu as pltpu
from jax.sharding import PartitionSpec as P

EDGE = 24
WINDOW = 112
FIRST = 80
SECOND = 64
BLOCK = 48
REST = 32
SLAB = 64
WIDE = 256
DEEP = 640
CURVE = 0.7978845608028654
CUBIC = 0.044715


def routed(block, axis, distance, closed):
    count = lax.axis_size(axis)
    if closed:
        route = [(i, (i + distance) % count) for i in range(count)]
    else:
        route = [(i, i + distance) for i in range(count) if 0 <= i + distance < count]
    return lax.ppermute(block, axis, route)


def gelu_slope(x):
    squared = x * x
    bend = jnp.tanh(CURVE * (x + CUBIC * x * squared))
    inner = CURVE * (1.0 + 3.0 * CUBIC * squared)
    return 0.5 * (1.0 + bend) + 0.5 * x * (1.0 - bend * bend) * inner


def table_kernel(ahead, behind, table, adjoint):
    kernels = ahead.shape[1]
    bf16 = jnp.bfloat16

    def sloped(row, lines, start):
        return pltpu.roll(
            jnp.broadcast_to(row, (lines, 128)), start, 1, stride=1, stride_axis=0
        )

    def forward(r, carry):
        for k in range(kernels):
            for part in (slice(0, 128), slice(128, 256)):
                table[r * kernels + k, :, part] = sloped(
                    ahead[r, k : k + 1, part], BLOCK, 0
                ).astype(bf16)
        return carry

    lax.fori_loop(0, ahead.shape[0], forward, 0)
    low = lax.broadcasted_iota(jnp.int32, (FIRST, 128), 1) < SECOND

    def backward(i, carry):
        for pair in range(DEEP // 128):
            k = 2 * pair
            even = sloped(behind[i, k : k + 1, :], FIRST, SECOND)
            if k + 1 < kernels:
                odd = sloped(behind[i, k + 1 : k + 2, :], FIRST, 0)
            else:
                odd = jnp.zeros_like(even)
            adjoint[i, :, pair * 128 : (pair + 1) * 128] = jnp.where(low, even, odd).astype(bf16)
        return carry

    lax.fori_loop(0, behind.shape[0], backward, 0)


def band_tables(ahead, behind):
    whole = pl.BlockSpec(memory_space=pltpu.VMEM)
    lines, kernels = ahead.shape[:2]
    return pl.pallas_call(
        table_kernel,
        out_shape=(
            jax.ShapeDtypeStruct((lines * kernels, BLOCK, WIDE), jnp.bfloat16),
            jax.ShapeDtypeStruct((behind.shape[0], FIRST, DEEP), jnp.bfloat16),
        ),
        in_specs=[whole] * 2,
        out_specs=(whole, whole),
        compiler_params=pltpu.CompilerParams(vmem_limit_bytes=16 * 1024 * 1024),
        name="tables",
    )(ahead, behind)


def device_kernel(
    flags,
    table,
    adjoint,
    field,
    own_matrix,
    other_near,
    other_far,
    section,
    keep,
    give,
    matrices,
    turned,
    basis0,
    basis1,
    middle,
    preact0,
    units1,
    spread,
    chosen_basis,
    chosen_units,
    grads,
):
    f32, bf16 = jnp.float32, jnp.bfloat16
    rows, chans = own_matrix.shape
    kernels = rows // chans
    half = rows // 2
    segment, core = flags[0], flags[1]
    lond = section.shape[2]
    near_start = pl.multiple_of(core * half, half)
    far_start = pl.multiple_of((1 - core) * half, half)

    def convolve(m, r, line, source, basis, start, pieces):
        for offset, count in pieces:
            blocks = [source[m, r + min(a, 2), offset : offset + SLAB] for a in range(4)]
            slab = jnp.concatenate(blocks, axis=0)
            rows_of = table[pl.ds(line * kernels, kernels), :count].reshape(kernels * count, WIDE)
            out = jnp.dot(rows_of, slab, preferred_element_type=f32)
            place = pl.multiple_of(start + offset, 16)
            for k in range(kernels):
                basis[pl.ds(place, count), k * chans : (k + 1) * chans] = out[
                    k * count : (k + 1) * count
                ].astype(bf16)

    def first_basis(r, carry):
        for m in range(2):
            convolve(m, r, r, field, basis0, (m * 6 + r) * FIRST, ((0, BLOCK), (BLOCK, REST)))
        return carry

    lax.fori_loop(0, 6, first_basis, 0, unroll=True)

    matrices[segment] = own_matrix[...]
    matrices[1 - segment, pl.ds(near_start, half)] = other_near[...]
    matrices[1 - segment, pl.ds(far_start, half)] = other_far[...]

    for k in range(kernels):
        span = slice(k * chans, (k + 1) * chans)
        turned[:, span] = jnp.transpose(matrices[1, span, :])

    def first_mix(m, carry):
        start = pl.multiple_of(m * 6 * FIRST, 16)
        pre = jnp.dot(
            basis0[pl.ds(start, 6 * FIRST), :], matrices[0], preferred_element_type=f32
        )
        centre = field[m, 1:7].astype(f32)[:, 8 : 8 + FIRST].reshape(6 * FIRST, chans)
        out = centre + jax.nn.gelu(pre)
        middle[m, :, :FIRST] = out.astype(bf16).reshape(6, FIRST, chans)
        middle[m, :, FIRST:] = jnp.zeros((6, 16, chans), bf16)
        for p in range(2):
            preact0[m, p] = pre[(p + 2) * FIRST + 16 : (p + 3) * FIRST]
        return carry

    lax.fori_loop(0, 2, first_mix, 0, unroll=True)

    def second_basis(s, carry):
        for m in range(2):
            start = (m * 4 + s) * SECOND
            convolve(m, s, s + 1, middle, basis1, start, ((0, REST), (REST, REST)))
        return carry

    lax.fori_loop(0, 4, second_basis, 0, unroll=True)

    def second_mix(m, carry):
        start = pl.multiple_of(m * 4 * SECOND, 4 * SECOND)
        pre = jnp.dot(
            basis1[pl.ds(start, 4 * SECOND), :], matrices[1], preferred_element_type=f32
        )
        incoming = field[m, 8:12, 16 : 16 + SECOND].astype(f32).reshape(4 * SECOND, chans)
        units1[pl.ds(start, 4 * SECOND), :] = (incoming * gelu_slope(pre)).astype(bf16)
        for p in range(2):
            own = middle[m, p + 2, 16 : 16 + SECOND].astype(f32)[:lond]
            begin = (p + 1) * SECOND + 8
            late = own + jax.nn.gelu(pre[begin : begin + lond])
            section[m, p] = jnp.where(segment == 0, own, late).astype(bf16)
        return carry

    lax.fori_loop(0, 2, second_mix, 0, unroll=True)

    column = lax.broadcasted_iota(jnp.int32, (SECOND, chans), 0)

    @pl.when(segment == 0)
    def _():
        live = column < lond
        spread[:, kernels * SECOND :, :] = jnp.zeros(
            (4, DEEP - kernels * SECOND, 2 * chans), bf16
        )
        for k in range(kernels):
            mixed = lax.dot_general(
                units1[...],
                turned[:, k * chans : (k + 1) * chans],
                (((1,), (0,)), ((), ())),
                preferred_element_type=f32,
            ).astype(bf16)
            for m in range(2):
                for s in range(4):
                    begin = (m * 4 + s) * SECOND
                    spread[
                        s, k * SECOND : (k + 1) * SECOND, m * chans : (m + 1) * chans
                    ] = mixed[begin : begin + SECOND]
        for p in range(2):
            back = jnp.zeros((FIRST, 2 * chans), f32)
            for a in range(3):
                s = p + 2 - a
                back += jnp.dot(adjoint[s * 3 + a], spread[s], preferred_element_type=f32)
            for m in range(2):
                place = (m * 2 + p) * SECOND
                total = field[m, 9 + p].astype(f32)[EDGE : EDGE + SECOND] + back[
                    16 : 16 + SECOND, m * chans : (m + 1) * chans
                ]
                grad = total.astype(bf16).astype(f32)
                unit = grad * gelu_slope(preact0[m, p])
                chosen_units[place : place + SECOND, :] = jnp.where(live, unit, 0.0).astype(bf16)
                begin = (m * 6 + p + 2) * FIRST + 16
                chosen_basis[place : place + SECOND, :] = basis0[begin : begin + SECOND, :]

    @pl.when(segment != 0)
    def _():
        live = (column >= 8) & (column < 8 + lond)
        for p in range(2):
            for m in range(2):
                place = (m * 2 + p) * SECOND
                begin = (m * 4 + p + 1) * SECOND
                unit = units1[begin : begin + SECOND, :].astype(f32)
                chosen_units[place : place + SECOND, :] = jnp.where(live, unit, 0.0).astype(bf16)
                chosen_basis[place : place + SECOND, :] = basis1[begin : begin + SECOND, :]

    for k in range(kernels):
        grads[k * chans : (k + 1) * chans, :] = lax.dot_general(
            chosen_basis[:, k * chans : (k + 1) * chans],
            chosen_units[...],
            (((0,), (0,)), ((), ())),
            preferred_element_type=f32,
        )
    keep[...] = grads[pl.ds(near_start, half), :]
    give[...] = grads[pl.ds(far_start, half), :].astype(bf16)


def on_device(flags, tables, field, own_matrix, other_near, other_far, lond):
    rows, chans = own_matrix.shape
    half = rows // 2
    bf16, f32 = jnp.bfloat16, jnp.float32
    whole = pl.BlockSpec(memory_space=pltpu.VMEM)
    return pl.pallas_call(
        device_kernel,
        out_shape=(
            jax.ShapeDtypeStruct((2, 2, lond, chans), bf16),
            jax.ShapeDtypeStruct((half, chans), f32),
            jax.ShapeDtypeStruct((half, chans), bf16),
        ),
        in_specs=[pl.BlockSpec(memory_space=pltpu.SMEM)] + [whole] * 6,
        out_specs=(whole, whole, whole),
        scratch_shapes=[
            pltpu.VMEM((2, rows, chans), bf16),
            pltpu.VMEM((chans, rows), bf16),
            pltpu.VMEM((12 * FIRST, rows), bf16),
            pltpu.VMEM((8 * SECOND, rows), bf16),
            pltpu.VMEM((2, 6, FIRST + 16, chans), bf16),
            pltpu.VMEM((2, 2, SECOND, chans), f32),
            pltpu.VMEM((8 * SECOND, chans), bf16),
            pltpu.VMEM((4, DEEP, 2 * chans), bf16),
            pltpu.VMEM((4 * SECOND, rows), bf16),
            pltpu.VMEM((4 * SECOND, chans), bf16),
            pltpu.VMEM((rows, chans), f32),
        ],
        compiler_params=pltpu.CompilerParams(vmem_limit_bytes=32 * 1024 * 1024),
        name="sphere",
    )(flags, *tables, field, own_matrix, other_near, other_far)


def gathered_sum(keep, give):
    lats, lons = lax.axis_size("lat"), lax.axis_size("lon")
    half, chans = keep.shape
    depth = 16
    planes = lons // depth
    columns = lats // 2 * planes
    swap = [(i, i ^ 1) for i in range(lats)]
    near = [
        [(2 * y + core) * lons + x * depth + z for y in range(lats // 2) for x in range(planes)]
        for core in range(2)
        for z in range(depth)
    ]
    far = [[x * depth + z for z in range(depth)] for x in range(planes)]
    core = lax.axis_index("lat") % 2
    own = (keep + lax.ppermute(give, "lat", swap).astype(jnp.float32)).astype(jnp.bfloat16)
    own = own.reshape(columns, half // columns, chans)
    own = lax.all_to_all(own, ("lat", "lon"), 0, 0, axis_index_groups=near)
    own = jnp.sum(own.astype(jnp.float32), axis=0).astype(jnp.bfloat16)
    own = own.reshape(depth, half // columns // depth, chans)
    own = lax.all_to_all(own, "lon", 0, 0, axis_index_groups=far)
    own = jnp.sum(own.astype(jnp.float32), axis=0).astype(jnp.bfloat16)
    own = jnp.broadcast_to(own[None], (depth,) + own.shape)
    own = lax.all_to_all(own, "lon", 0, 0, axis_index_groups=far).reshape(-1, chans)
    own = jnp.broadcast_to(own[None], (columns,) + own.shape)
    own = lax.all_to_all(own, ("lat", "lon"), 0, 0, axis_index_groups=near).reshape(-1, chans)
    other = lax.ppermute(own, "lat", swap)
    first = jnp.where(core == 0, own, other)
    second = jnp.where(core == 0, other, own)
    return jnp.concatenate([first, second], axis=0).astype(jnp.float32)


def tap_rows(psi, band_half, lat_start):
    kernels, lines, offsets, width = psi.shape
    taps = lax.broadcasted_iota(jnp.int32, psi.shape, 3)
    live = jnp.abs(taps - (width - 1) // 2) <= band_half[None, :, :, None]
    effective = jnp.where(live, psi, jnp.zeros_like(psi)).astype(jnp.float32)
    by_row = jnp.transpose(effective, (1, 0, 2, 3))
    by_row = jnp.pad(by_row, ((2, 2), (0, 0), (0, 0), (0, 0)))
    own = lax.dynamic_slice_in_dim(by_row, lat_start, 6, 0)
    ahead = jnp.pad(own, ((0, 0), (0, 0), (0, 1), (0, SLAB - width)))
    ahead = ahead.reshape(6, kernels, WIDE)
    behind = jnp.transpose(jnp.flip(own[1:5], 3), (0, 2, 1, 3))
    start = SECOND - width + 1
    behind = jnp.pad(behind, ((0, 0), (0, 0), (0, 0), (start, 128 - width - start)))
    return ahead, behind.reshape(4 * offsets, kernels, 128)


def across():
    lons = lax.axis_size("lon")
    depth = lons // 2
    return [
        (seg * lons + x * depth + z, (1 - seg) * lons + (1 - x) * depth + z)
        for seg in range(2)
        for x in range(2)
        for z in range(depth)
    ]


def widened(inputs, cotangent):
    lond = inputs.shape[2]
    both = jnp.concatenate([inputs, cotangent[:, 1:]], axis=1)
    down = routed(both, "lat", 1, False)
    both = jnp.concatenate([inputs, cotangent[:, :1]], axis=1)
    up = routed(both, "lat", -1, False)
    down_far = routed(inputs[:, 1:], "lat", 2, False)
    up_far = routed(inputs[:, :1], "lat", -2, False)
    lines = jnp.concatenate(
        [
            down_far,
            down[:, :2],
            inputs,
            up[:, :2],
            up_far,
            down[:, 2:],
            cotangent,
            up[:, 2:],
        ],
        axis=1,
    )
    left = routed(lines[:, :, lond - EDGE :], "lon", 1, True)
    right = routed(lines[:, :, :EDGE], "lon", -1, True)
    return lines, left, right


def joined(left, lines, right):
    lond = lines.shape[2]
    blank = jnp.zeros(lines.shape[:2] + (WINDOW - lond - 2 * EDGE, lines.shape[3]), lines.dtype)
    return jnp.concatenate([left, lines, right, blank], axis=2)


def shards(inputs, cotangent, weights, psi, band_half):
    lat = lax.axis_index("lat")
    core = lat % 2
    segment = lax.axis_index("segment")
    matrix = weights[0]
    half = matrix.shape[0] // 2
    mine = lax.dynamic_slice_in_dim(matrix, core * half, half, 0)
    other_near = lax.ppermute(mine, ("segment", "lon"), across())
    lines, left, right = widened(inputs, cotangent)
    tables = band_tables(*tap_rows(psi, band_half, lat * inputs.shape[1]))
    left, right, other_near, tables = lax.optimization_barrier((left, right, other_near, tables))
    other_far = lax.ppermute(
        other_near, "lat", [(i, i ^ 1) for i in range(lax.axis_size("lat"))]
    )
    field = joined(left, lines, right)
    flags = jnp.stack([segment, core]).astype(jnp.int32)
    section, keep, give = on_device(
        flags, tables, field, matrix, other_near, other_far, inputs.shape[2]
    )
    return (section[None], gathered_sum(keep, give)[None])


def solution(mesh):
    placed = (
        P(None, "lat", "lon", None),
        P(None, "lat", "lon", None),
        P("segment", None, None),
        P(),
        P(),
    )
    return jax.shard_map(
        shards,
        mesh=mesh,
        in_specs=placed,
        out_specs=(P("segment", None, "lat", "lon", None), P("segment", None, None)),
        check_vma=False,
    )
```

```python
import functools

import jax
import jax.numpy as jnp
from jax import lax
from jax.experimental import pallas as pl
from jax.experimental.pallas import tpu as pltpu
from jax.sharding import PartitionSpec as P

EDGE = 24
WINDOW = 112
FIRST = 80
SECOND = 64
BLOCK = 48
REST = 32
SLAB = 64
WIDE = 256
DEEP = 640
CURVE = 0.7978845608028654
CUBIC = 0.044715


def routed(block, axis, distance, closed):
    count = lax.axis_size(axis)
    if closed:
        route = [(i, (i + distance) % count) for i in range(count)]
    else:
        route = [(i, i + distance) for i in range(count) if 0 <= i + distance < count]
    return lax.ppermute(block, axis, route)


def gelu_slope(x):
    squared = x * x
    bend = jnp.tanh(CURVE * (x + CUBIC * x * squared))
    inner = CURVE * (1.0 + 3.0 * CUBIC * squared)
    return 0.5 * (1.0 + bend) + 0.5 * x * (1.0 - bend * bend) * inner


def table_kernel(ahead, behind, table, adjoint):
    kernels = ahead.shape[1]
    bf16 = jnp.bfloat16

    def sloped(row, lines, start):
        return pltpu.roll(
            jnp.broadcast_to(row, (lines, 128)), start, 1, stride=1, stride_axis=0
        )

    def forward(r, carry):
        for k in range(kernels):
            for part in (slice(0, 128), slice(128, 256)):
                table[r * kernels + k, :, part] = sloped(
                    ahead[r, k : k + 1, part], BLOCK, 0
                ).astype(bf16)
        return carry

    lax.fori_loop(0, ahead.shape[0], forward, 0)
    low = lax.broadcasted_iota(jnp.int32, (FIRST, 128), 1) < SECOND

    def backward(i, carry):
        for pair in range(DEEP // 128):
            k = 2 * pair
            even = sloped(behind[i, k : k + 1, :], FIRST, SECOND)
            if k + 1 < kernels:
                odd = sloped(behind[i, k + 1 : k + 2, :], FIRST, 0)
            else:
                odd = jnp.zeros_like(even)
            adjoint[i, :, pair * 128 : (pair + 1) * 128] = jnp.where(low, even, odd).astype(bf16)
        return carry

    lax.fori_loop(0, behind.shape[0], backward, 0)


def band_tables(ahead, behind):
    whole = pl.BlockSpec(memory_space=pltpu.VMEM)
    lines, kernels = ahead.shape[:2]
    return pl.pallas_call(
        table_kernel,
        out_shape=(
            jax.ShapeDtypeStruct((lines * kernels, BLOCK, WIDE), jnp.bfloat16),
            jax.ShapeDtypeStruct((behind.shape[0], FIRST, DEEP), jnp.bfloat16),
        ),
        in_specs=[whole] * 2,
        out_specs=(whole, whole),
        compiler_params=pltpu.CompilerParams(vmem_limit_bytes=16 * 1024 * 1024),
        name="tables",
    )(ahead, behind)


def device_kernel(
    flags,
    table,
    adjoint,
    field,
    own_matrix,
    other_near,
    other_far,
    section,
    keep,
    give,
    matrices,
    turned,
    basis0,
    basis1,
    middle,
    preact0,
    units1,
    spread,
    chosen_basis,
    chosen_units,
    grads,
):
    f32, bf16 = jnp.float32, jnp.bfloat16
    rows, chans = own_matrix.shape
    kernels = rows // chans
    half = rows // 2
    segment, core = flags[0], flags[1]
    lond = section.shape[2]
    near_start = pl.multiple_of(core * half, half)
    far_start = pl.multiple_of((1 - core) * half, half)

    def convolve(m, r, line, source, basis, start, pieces):
        for offset, count in pieces:
            blocks = [source[m, r + min(a, 2), offset : offset + SLAB] for a in range(4)]
            slab = jnp.concatenate(blocks, axis=0)
            rows_of = table[pl.ds(line * kernels, kernels), :count].reshape(kernels * count, WIDE)
            out = jnp.dot(rows_of, slab, preferred_element_type=f32)
            place = pl.multiple_of(start + offset, 16)
            for k in range(kernels):
                basis[pl.ds(place, count), k * chans : (k + 1) * chans] = out[
                    k * count : (k + 1) * count
                ].astype(bf16)

    def first_basis(r, carry):
        for m in range(2):
            convolve(m, r, r, field, basis0, (m * 6 + r) * FIRST, ((0, BLOCK), (BLOCK, REST)))
        return carry

    lax.fori_loop(0, 6, first_basis, 0, unroll=True)

    matrices[segment] = own_matrix[...]
    matrices[1 - segment, pl.ds(near_start, half)] = other_near[...]
    matrices[1 - segment, pl.ds(far_start, half)] = other_far[...]

    for k in range(kernels):
        span = slice(k * chans, (k + 1) * chans)
        turned[:, span] = jnp.transpose(matrices[1, span, :])

    def first_mix(m, carry):
        start = pl.multiple_of(m * 6 * FIRST, 16)
        pre = jnp.dot(
            basis0[pl.ds(start, 6 * FIRST), :], matrices[0], preferred_element_type=f32
        )
        centre = field[m, 1:7].astype(f32)[:, 8 : 8 + FIRST].reshape(6 * FIRST, chans)
        out = centre + jax.nn.gelu(pre)
        middle[m, :, :FIRST] = out.astype(bf16).reshape(6, FIRST, chans)
        middle[m, :, FIRST:] = jnp.zeros((6, 16, chans), bf16)
        for p in range(2):
            preact0[m, p] = pre[(p + 2) * FIRST + 16 : (p + 3) * FIRST]
        return carry

    lax.fori_loop(0, 2, first_mix, 0, unroll=True)

    def second_basis(s, carry):
        for m in range(2):
            start = (m * 4 + s) * SECOND
            convolve(m, s, s + 1, middle, basis1, start, ((0, REST), (REST, REST)))
        return carry

    lax.fori_loop(0, 4, second_basis, 0, unroll=True)

    def second_mix(m, carry):
        start = pl.multiple_of(m * 4 * SECOND, 4 * SECOND)
        pre = jnp.dot(
            basis1[pl.ds(start, 4 * SECOND), :], matrices[1], preferred_element_type=f32
        )
        incoming = field[m, 8:12, 16 : 16 + SECOND].astype(f32).reshape(4 * SECOND, chans)
        units1[pl.ds(start, 4 * SECOND), :] = (incoming * gelu_slope(pre)).astype(bf16)
        for p in range(2):
            own = middle[m, p + 2, 16 : 16 + SECOND].astype(f32)[:lond]
            begin = (p + 1) * SECOND + 8
            late = own + jax.nn.gelu(pre[begin : begin + lond])
            section[m, p] = jnp.where(segment == 0, own, late).astype(bf16)
        return carry

    lax.fori_loop(0, 2, second_mix, 0, unroll=True)

    column = lax.broadcasted_iota(jnp.int32, (SECOND, chans), 0)

    @pl.when(segment == 0)
    def _():
        live = column < lond
        spread[:, kernels * SECOND :, :] = jnp.zeros(
            (4, DEEP - kernels * SECOND, 2 * chans), bf16
        )
        for k in range(kernels):
            mixed = lax.dot_general(
                units1[...],
                turned[:, k * chans : (k + 1) * chans],
                (((1,), (0,)), ((), ())),
                preferred_element_type=f32,
            ).astype(bf16)
            for m in range(2):
                for s in range(4):
                    begin = (m * 4 + s) * SECOND
                    spread[
                        s, k * SECOND : (k + 1) * SECOND, m * chans : (m + 1) * chans
                    ] = mixed[begin : begin + SECOND]
        for p in range(2):
            back = jnp.zeros((FIRST, 2 * chans), f32)
            for a in range(3):
                s = p + 2 - a
                back += jnp.dot(adjoint[s * 3 + a], spread[s], preferred_element_type=f32)
            for m in range(2):
                place = (m * 2 + p) * SECOND
                total = field[m, 9 + p].astype(f32)[EDGE : EDGE + SECOND] + back[
                    16 : 16 + SECOND, m * chans : (m + 1) * chans
                ]
                grad = total.astype(bf16).astype(f32)
                unit = grad * gelu_slope(preact0[m, p])
                chosen_units[place : place + SECOND, :] = jnp.where(live, unit, 0.0).astype(bf16)
                begin = (m * 6 + p + 2) * FIRST + 16
                chosen_basis[place : place + SECOND, :] = basis0[begin : begin + SECOND, :]

    @pl.when(segment != 0)
    def _():
        live = (column >= 8) & (column < 8 + lond)
        for p in range(2):
            for m in range(2):
                place = (m * 2 + p) * SECOND
                begin = (m * 4 + p + 1) * SECOND
                unit = units1[begin : begin + SECOND, :].astype(f32)
                chosen_units[place : place + SECOND, :] = jnp.where(live, unit, 0.0).astype(bf16)
                chosen_basis[place : place + SECOND, :] = basis1[begin : begin + SECOND, :]

    for k in range(kernels):
        grads[k * chans : (k + 1) * chans, :] = lax.dot_general(
            chosen_basis[:, k * chans : (k + 1) * chans],
            chosen_units[...],
            (((0,), (0,)), ((), ())),
            preferred_element_type=f32,
        )
    keep[...] = grads[pl.ds(near_start, half), :]
    give[...] = grads[pl.ds(far_start, half), :].astype(bf16)


def on_device(flags, tables, field, own_matrix, other_near, other_far, lond):
    rows, chans = own_matrix.shape
    half = rows // 2
    bf16, f32 = jnp.bfloat16, jnp.float32
    whole = pl.BlockSpec(memory_space=pltpu.VMEM)
    return pl.pallas_call(
        device_kernel,
        out_shape=(
            jax.ShapeDtypeStruct((2, 2, lond, chans), bf16),
            jax.ShapeDtypeStruct((half, chans), f32),
            jax.ShapeDtypeStruct((half, chans), bf16),
        ),
        in_specs=[pl.BlockSpec(memory_space=pltpu.SMEM)] + [whole] * 6,
        out_specs=(whole, whole, whole),
        scratch_shapes=[
            pltpu.VMEM((2, rows, chans), bf16),
            pltpu.VMEM((chans, rows), bf16),
            pltpu.VMEM((12 * FIRST, rows), bf16),
            pltpu.VMEM((8 * SECOND, rows), bf16),
            pltpu.VMEM((2, 6, FIRST + 16, chans), bf16),
            pltpu.VMEM((2, 2, SECOND, chans), f32),
            pltpu.VMEM((8 * SECOND, chans), bf16),
            pltpu.VMEM((4, DEEP, 2 * chans), bf16),
            pltpu.VMEM((4 * SECOND, rows), bf16),
            pltpu.VMEM((4 * SECOND, chans), bf16),
            pltpu.VMEM((rows, chans), f32),
        ],
        compiler_params=pltpu.CompilerParams(vmem_limit_bytes=32 * 1024 * 1024),
        name="sphere",
    )(flags, *tables, field, own_matrix, other_near, other_far)


def gathered_sum(keep, give):
    lats, lons = lax.axis_size("lat"), lax.axis_size("lon")
    half, chans = keep.shape
    depth = 16
    planes = lons // depth
    columns = lats // 2 * planes
    swap = [(i, i ^ 1) for i in range(lats)]
    near = [
        [(2 * y + core) * lons + x * depth + z for y in range(lats // 2) for x in range(planes)]
        for core in range(2)
        for z in range(depth)
    ]
    hop = 4
    beside = [[b + i for i in range(hop)] for b in range(0, lons, hop)]
    apart = [
        [x * depth + b + i * hop for i in range(depth // hop)]
        for x in range(planes)
        for b in range(hop)
    ]
    core = lax.axis_index("lat") % 2
    own = (keep + lax.ppermute(give, "lat", swap).astype(jnp.float32)).astype(jnp.bfloat16)
    own = own.reshape(columns, half // columns, chans)
    own = lax.all_to_all(own, ("lat", "lon"), 0, 0, axis_index_groups=near)
    own = jnp.sum(own.astype(jnp.float32), axis=0).astype(jnp.bfloat16)
    lines, lanes = half // columns // 2, chans // 2
    own = own.reshape(2, lines, 2, lanes).transpose(0, 2, 1, 3).reshape(hop, lines, lanes)
    own = lax.all_to_all(own, "lon", 0, 0, axis_index_groups=beside)
    own = jnp.sum(own.astype(jnp.float32), axis=0).astype(jnp.bfloat16)
    own = jnp.broadcast_to(own[None], (depth // hop,) + own.shape)
    own = lax.all_to_all(own, "lon", 0, 0, axis_index_groups=apart)
    own = jnp.sum(own.astype(jnp.float32), axis=0).astype(jnp.bfloat16)
    own = jnp.broadcast_to(own[None], (hop,) + own.shape)
    own = lax.all_to_all(own, "lon", 0, 0, axis_index_groups=beside)
    own = own.reshape(2, 2, lines, lanes).transpose(0, 2, 1, 3).reshape(2 * lines, chans)
    own = jnp.broadcast_to(own[None], (columns,) + own.shape)
    own = lax.all_to_all(own, ("lat", "lon"), 0, 0, axis_index_groups=near).reshape(-1, chans)
    other = lax.ppermute(own, "lat", swap)
    first = jnp.where(core == 0, own, other)
    second = jnp.where(core == 0, other, own)
    return jnp.concatenate([first, second], axis=0).astype(jnp.float32)


def tap_rows(psi, band_half, lat_start):
    kernels, lines, offsets, width = psi.shape
    taps = lax.broadcasted_iota(jnp.int32, psi.shape, 3)
    live = jnp.abs(taps - (width - 1) // 2) <= band_half[None, :, :, None]
    effective = jnp.where(live, psi, jnp.zeros_like(psi)).astype(jnp.float32)
    by_row = jnp.transpose(effective, (1, 0, 2, 3))
    by_row = jnp.pad(by_row, ((2, 2), (0, 0), (0, 0), (0, 0)))
    own = lax.dynamic_slice_in_dim(by_row, lat_start, 6, 0)
    ahead = jnp.pad(own, ((0, 0), (0, 0), (0, 1), (0, SLAB - width)))
    ahead = ahead.reshape(6, kernels, WIDE)
    behind = jnp.transpose(jnp.flip(own[1:5], 3), (0, 2, 1, 3))
    start = SECOND - width + 1
    behind = jnp.pad(behind, ((0, 0), (0, 0), (0, 0), (start, 128 - width - start)))
    return ahead, behind.reshape(4 * offsets, kernels, 128)


def across():
    lons = lax.axis_size("lon")
    depth = lons // 2
    return [
        (seg * lons + x * depth + z, (1 - seg) * lons + (1 - x) * depth + z)
        for seg in range(2)
        for x in range(2)
        for z in range(depth)
    ]


def widened(inputs, cotangent):
    lond = inputs.shape[2]
    both = jnp.concatenate([inputs, cotangent[:, 1:]], axis=1)
    down = routed(both, "lat", 1, False)
    both = jnp.concatenate([inputs, cotangent[:, :1]], axis=1)
    up = routed(both, "lat", -1, False)
    down_far = routed(inputs[:, 1:], "lat", 2, False)
    up_far = routed(inputs[:, :1], "lat", -2, False)
    lines = jnp.concatenate(
        [
            down_far,
            down[:, :2],
            inputs,
            up[:, :2],
            up_far,
            down[:, 2:],
            cotangent,
            up[:, 2:],
        ],
        axis=1,
    )
    left = routed(lines[:, :, lond - EDGE :], "lon", 1, True)
    right = routed(lines[:, :, :EDGE], "lon", -1, True)
    return lines, left, right


def joined(left, lines, right):
    lond = lines.shape[2]
    blank = jnp.zeros(lines.shape[:2] + (WINDOW - lond - 2 * EDGE, lines.shape[3]), lines.dtype)
    return jnp.concatenate([left, lines, right, blank], axis=2)


def shards(inputs, cotangent, weights, psi, band_half):
    lat = lax.axis_index("lat")
    core = lat % 2
    segment = lax.axis_index("segment")
    matrix = weights[0]
    half = matrix.shape[0] // 2
    mine = lax.dynamic_slice_in_dim(matrix, core * half, half, 0)
    other_near = lax.ppermute(mine, ("segment", "lon"), across())
    lines, left, right = widened(inputs, cotangent)
    tables = band_tables(*tap_rows(psi, band_half, lat * inputs.shape[1]))
    left, right, other_near, tables = lax.optimization_barrier((left, right, other_near, tables))
    other_far = lax.ppermute(
        other_near, "lat", [(i, i ^ 1) for i in range(lax.axis_size("lat"))]
    )
    field = joined(left, lines, right)
    flags = jnp.stack([segment, core]).astype(jnp.int32)
    section, keep, give = on_device(
        flags, tables, field, matrix, other_near, other_far, inputs.shape[2]
    )
    return (section[None], gathered_sum(keep, give)[None])


def solution(mesh):
    placed = (
        P(None, "lat", "lon", None),
        P(None, "lat", "lon", None),
        P("segment", None, None),
        P(),
        P(),
    )
    return jax.shard_map(
        shards,
        mesh=mesh,
        in_specs=placed,
        out_specs=(P("segment", None, "lat", "lon", None), P("segment", None, None)),
        check_vma=False,
    )
```

```python
import functools

import jax
import jax.numpy as jnp
from jax import lax
from jax.experimental import pallas as pl
from jax.experimental.pallas import tpu as pltpu
from jax.sharding import PartitionSpec as P

EDGE = 24
WINDOW = 112
FIRST = 80
SECOND = 64
BLOCK = 48
REST = 32
SLAB = 64
WIDE = 256
DEEP = 640
CURVE = 0.7978845608028654
CUBIC = 0.044715


def routed(block, axis, distance, closed):
    count = lax.axis_size(axis)
    if closed:
        route = [(i, (i + distance) % count) for i in range(count)]
    else:
        route = [(i, i + distance) for i in range(count) if 0 <= i + distance < count]
    return lax.ppermute(block, axis, route)


def gelu_slope(x):
    squared = x * x
    bend = jnp.tanh(CURVE * (x + CUBIC * x * squared))
    inner = CURVE * (1.0 + 3.0 * CUBIC * squared)
    return 0.5 * (1.0 + bend) + 0.5 * x * (1.0 - bend * bend) * inner


def table_kernel(ahead, behind, table, adjoint):
    kernels = ahead.shape[1]
    bf16 = jnp.bfloat16

    def sloped(row, lines, start):
        return pltpu.roll(
            jnp.broadcast_to(row, (lines, 128)), start, 1, stride=1, stride_axis=0
        )

    def forward(r, carry):
        for k in range(kernels):
            for part in (slice(0, 128), slice(128, 256)):
                table[r * kernels + k, :, part] = sloped(
                    ahead[r, k : k + 1, part], BLOCK, 0
                ).astype(bf16)
        return carry

    lax.fori_loop(0, ahead.shape[0], forward, 0)
    low = lax.broadcasted_iota(jnp.int32, (FIRST, 128), 1) < SECOND

    def backward(i, carry):
        for pair in range(DEEP // 128):
            k = 2 * pair
            even = sloped(behind[i, k : k + 1, :], FIRST, SECOND)
            if k + 1 < kernels:
                odd = sloped(behind[i, k + 1 : k + 2, :], FIRST, 0)
            else:
                odd = jnp.zeros_like(even)
            adjoint[i, :, pair * 128 : (pair + 1) * 128] = jnp.where(low, even, odd).astype(bf16)
        return carry

    lax.fori_loop(0, behind.shape[0], backward, 0)


def band_tables(ahead, behind):
    whole = pl.BlockSpec(memory_space=pltpu.VMEM)
    lines, kernels = ahead.shape[:2]
    return pl.pallas_call(
        table_kernel,
        out_shape=(
            jax.ShapeDtypeStruct((lines * kernels, BLOCK, WIDE), jnp.bfloat16),
            jax.ShapeDtypeStruct((behind.shape[0], FIRST, DEEP), jnp.bfloat16),
        ),
        in_specs=[whole] * 2,
        out_specs=(whole, whole),
        compiler_params=pltpu.CompilerParams(vmem_limit_bytes=16 * 1024 * 1024),
        name="tables",
    )(ahead, behind)


def device_kernel(
    flags,
    table,
    adjoint,
    field,
    own_matrix,
    other_near,
    other_far,
    section,
    keep,
    give,
    matrices,
    turned,
    basis0,
    basis1,
    middle,
    preact0,
    units1,
    spread,
    chosen_basis,
    chosen_units,
    grads,
):
    f32, bf16 = jnp.float32, jnp.bfloat16
    rows, chans = own_matrix.shape
    kernels = rows // chans
    half = rows // 2
    segment, core = flags[0], flags[1]
    lond = section.shape[2]
    near_start = pl.multiple_of(core * half, half)
    far_start = pl.multiple_of((1 - core) * half, half)

    def convolve(m, r, line, source, basis, start, pieces):
        for offset, count in pieces:
            blocks = [source[m, r + min(a, 2), offset : offset + SLAB] for a in range(4)]
            slab = jnp.concatenate(blocks, axis=0)
            rows_of = table[pl.ds(line * kernels, kernels), :count].reshape(kernels * count, WIDE)
            out = jnp.dot(rows_of, slab, preferred_element_type=f32)
            place = pl.multiple_of(start + offset, 16)
            for k in range(kernels):
                basis[pl.ds(place, count), k * chans : (k + 1) * chans] = out[
                    k * count : (k + 1) * count
                ].astype(bf16)

    def first_basis(r, carry):
        for m in range(2):
            convolve(m, r, r, field, basis0, (m * 6 + r) * FIRST, ((0, BLOCK), (BLOCK, REST)))
        return carry

    lax.fori_loop(0, 6, first_basis, 0, unroll=True)

    matrices[segment] = own_matrix[...]
    matrices[1 - segment, pl.ds(near_start, half)] = other_near[...]
    matrices[1 - segment, pl.ds(far_start, half)] = other_far[...]

    for k in range(kernels):
        span = slice(k * chans, (k + 1) * chans)
        turned[:, span] = jnp.transpose(matrices[1, span, :])

    def first_mix(m, carry):
        start = pl.multiple_of(m * 6 * FIRST, 16)
        pre = jnp.dot(
            basis0[pl.ds(start, 6 * FIRST), :], matrices[0], preferred_element_type=f32
        )
        centre = field[m, 1:7].astype(f32)[:, 8 : 8 + FIRST].reshape(6 * FIRST, chans)
        out = centre + jax.nn.gelu(pre)
        middle[m, :, :FIRST] = out.astype(bf16).reshape(6, FIRST, chans)
        middle[m, :, FIRST:] = jnp.zeros((6, 16, chans), bf16)
        for p in range(2):
            preact0[m, p] = pre[(p + 2) * FIRST + 16 : (p + 3) * FIRST]
        return carry

    lax.fori_loop(0, 2, first_mix, 0, unroll=True)

    def second_basis(s, carry):
        for m in range(2):
            start = (m * 4 + s) * SECOND
            convolve(m, s, s + 1, middle, basis1, start, ((0, REST), (REST, REST)))
        return carry

    lax.fori_loop(0, 4, second_basis, 0, unroll=True)

    def second_mix(m, carry):
        start = pl.multiple_of(m * 4 * SECOND, 4 * SECOND)
        pre = jnp.dot(
            basis1[pl.ds(start, 4 * SECOND), :], matrices[1], preferred_element_type=f32
        )
        incoming = field[m, 8:12, 16 : 16 + SECOND].astype(f32).reshape(4 * SECOND, chans)
        units1[pl.ds(start, 4 * SECOND), :] = (incoming * gelu_slope(pre)).astype(bf16)
        for p in range(2):
            own = middle[m, p + 2, 16 : 16 + SECOND].astype(f32)[:lond]
            begin = (p + 1) * SECOND + 8
            late = own + jax.nn.gelu(pre[begin : begin + lond])
            section[m, p] = jnp.where(segment == 0, own, late).astype(bf16)
        return carry

    lax.fori_loop(0, 2, second_mix, 0, unroll=True)

    column = lax.broadcasted_iota(jnp.int32, (SECOND, chans), 0)

    @pl.when(segment == 0)
    def _():
        live = column < lond
        spread[:, kernels * SECOND :, :] = jnp.zeros(
            (4, DEEP - kernels * SECOND, 2 * chans), bf16
        )
        for k in range(kernels):
            mixed = lax.dot_general(
                units1[...],
                turned[:, k * chans : (k + 1) * chans],
                (((1,), (0,)), ((), ())),
                preferred_element_type=f32,
            ).astype(bf16)
            for m in range(2):
                for s in range(4):
                    begin = (m * 4 + s) * SECOND
                    spread[
                        s, k * SECOND : (k + 1) * SECOND, m * chans : (m + 1) * chans
                    ] = mixed[begin : begin + SECOND]
        for p in range(2):
            back = jnp.zeros((FIRST, 2 * chans), f32)
            for a in range(3):
                s = p + 2 - a
                back += jnp.dot(adjoint[s * 3 + a], spread[s], preferred_element_type=f32)
            for m in range(2):
                place = (m * 2 + p) * SECOND
                total = field[m, 9 + p].astype(f32)[EDGE : EDGE + SECOND] + back[
                    16 : 16 + SECOND, m * chans : (m + 1) * chans
                ]
                grad = total.astype(bf16).astype(f32)
                unit = grad * gelu_slope(preact0[m, p])
                chosen_units[place : place + SECOND, :] = jnp.where(live, unit, 0.0).astype(bf16)
                begin = (m * 6 + p + 2) * FIRST + 16
                chosen_basis[place : place + SECOND, :] = basis0[begin : begin + SECOND, :]

    @pl.when(segment != 0)
    def _():
        live = (column >= 8) & (column < 8 + lond)
        for p in range(2):
            for m in range(2):
                place = (m * 2 + p) * SECOND
                begin = (m * 4 + p + 1) * SECOND
                unit = units1[begin : begin + SECOND, :].astype(f32)
                chosen_units[place : place + SECOND, :] = jnp.where(live, unit, 0.0).astype(bf16)
                chosen_basis[place : place + SECOND, :] = basis1[begin : begin + SECOND, :]

    for k in range(kernels):
        grads[k * chans : (k + 1) * chans, :] = lax.dot_general(
            chosen_basis[:, k * chans : (k + 1) * chans],
            chosen_units[...],
            (((0,), (0,)), ((), ())),
            preferred_element_type=f32,
        )
    keep[...] = grads[pl.ds(near_start, half), :]
    give[...] = grads[pl.ds(far_start, half), :].astype(bf16)


def on_device(flags, tables, field, own_matrix, other_near, other_far, lond):
    rows, chans = own_matrix.shape
    half = rows // 2
    bf16, f32 = jnp.bfloat16, jnp.float32
    whole = pl.BlockSpec(memory_space=pltpu.VMEM)
    return pl.pallas_call(
        device_kernel,
        out_shape=(
            jax.ShapeDtypeStruct((2, 2, lond, chans), bf16),
            jax.ShapeDtypeStruct((half, chans), f32),
            jax.ShapeDtypeStruct((half, chans), bf16),
        ),
        in_specs=[pl.BlockSpec(memory_space=pltpu.SMEM)] + [whole] * 6,
        out_specs=(whole, whole, whole),
        scratch_shapes=[
            pltpu.VMEM((2, rows, chans), bf16),
            pltpu.VMEM((chans, rows), bf16),
            pltpu.VMEM((12 * FIRST, rows), bf16),
            pltpu.VMEM((8 * SECOND, rows), bf16),
            pltpu.VMEM((2, 6, FIRST + 16, chans), bf16),
            pltpu.VMEM((2, 2, SECOND, chans), f32),
            pltpu.VMEM((8 * SECOND, chans), bf16),
            pltpu.VMEM((4, DEEP, 2 * chans), bf16),
            pltpu.VMEM((4 * SECOND, rows), bf16),
            pltpu.VMEM((4 * SECOND, chans), bf16),
            pltpu.VMEM((rows, chans), f32),
        ],
        compiler_params=pltpu.CompilerParams(vmem_limit_bytes=32 * 1024 * 1024),
        name="sphere",
    )(flags, *tables, field, own_matrix, other_near, other_far)


def gathered_sum(keep, give):
    lats, lons = lax.axis_size("lat"), lax.axis_size("lon")
    half, chans = keep.shape
    depth = 16
    planes = lons // depth
    columns = lats // 2 * planes
    swap = [(i, i ^ 1) for i in range(lats)]
    near = [
        [(2 * y + core) * lons + x * depth + z for y in range(lats // 2) for x in range(planes)]
        for core in range(2)
        for z in range(depth)
    ]
    hop = 4
    beside = [[b + i for i in range(hop)] for b in range(0, lons, hop)]
    apart = [
        [x * depth + b + i * hop for i in range(depth // hop)]
        for x in range(planes)
        for b in range(hop)
    ]
    core = lax.axis_index("lat") % 2
    own = (keep + lax.ppermute(give, "lat", swap).astype(jnp.float32)).astype(jnp.bfloat16)
    own = own.reshape(columns, half // columns, chans)
    own = lax.all_to_all(own, ("lat", "lon"), 0, 0, axis_index_groups=near)
    own = jnp.sum(own.astype(jnp.float32), axis=0).astype(jnp.bfloat16)
    lines, lanes = half // columns // 2, chans // 2
    own = own.reshape(2, lines, 2, lanes).transpose(0, 2, 1, 3).reshape(hop, lines, lanes)
    own = lax.all_to_all(own, "lon", 0, 0, axis_index_groups=beside)
    own = jnp.sum(own.astype(jnp.float32), axis=0).astype(jnp.bfloat16)
    own = jnp.broadcast_to(own[None], (depth // hop,) + own.shape)
    own = lax.all_to_all(own, "lon", 0, 0, axis_index_groups=apart)
    own = jnp.sum(own.astype(jnp.float32), axis=0).astype(jnp.bfloat16)
    own = jnp.broadcast_to(own[None], (hop,) + own.shape)
    own = lax.all_to_all(own, "lon", 0, 0, axis_index_groups=beside)
    own = own.reshape(2, 2, lines, lanes).transpose(0, 2, 1, 3).reshape(2 * lines, chans)
    own = jnp.broadcast_to(own[None], (columns,) + own.shape)
    own = lax.all_to_all(own, ("lat", "lon"), 0, 0, axis_index_groups=near).reshape(-1, chans)
    other = lax.ppermute(own, "lat", swap)
    first = jnp.where(core == 0, own, other)
    second = jnp.where(core == 0, other, own)
    return jnp.concatenate([first, second], axis=0).astype(jnp.float32)


def tap_rows(psi, band_half, lat_start):
    kernels, lines, offsets, width = psi.shape
    taps = lax.broadcasted_iota(jnp.int32, psi.shape, 3)
    live = jnp.abs(taps - (width - 1) // 2) <= band_half[None, :, :, None]
    effective = jnp.where(live, psi, jnp.zeros_like(psi)).astype(jnp.float32)
    by_row = jnp.transpose(effective, (1, 0, 2, 3))
    by_row = jnp.pad(by_row, ((2, 2), (0, 0), (0, 0), (0, 0)))
    own = lax.dynamic_slice_in_dim(by_row, lat_start, 6, 0)
    ahead = jnp.pad(own, ((0, 0), (0, 0), (0, 1), (0, SLAB - width)))
    ahead = ahead.reshape(6, kernels, WIDE)
    behind = jnp.transpose(jnp.flip(own[1:5], 3), (0, 2, 1, 3))
    start = SECOND - width + 1
    behind = jnp.pad(behind, ((0, 0), (0, 0), (0, 0), (start, 128 - width - start)))
    return ahead, behind.reshape(4 * offsets, kernels, 128)


def across():
    lons = lax.axis_size("lon")
    depth = lons // 2
    return [
        (seg * lons + x * depth + z, (1 - seg) * lons + (1 - x) * depth + z)
        for seg in range(2)
        for x in range(2)
        for z in range(depth)
    ]


def widened(inputs, cotangent):
    lond = inputs.shape[2]
    lats = lax.axis_size("lat")
    core = lax.axis_index("lat") % 2
    own = jnp.concatenate([inputs, cotangent], axis=1)
    mate = lax.ppermute(own, "lat", [(i, i ^ 1) for i in range(lats)])
    first = jnp.where(core == 0, own, mate)
    second = jnp.where(core == 0, mate, own)
    up = routed(
        jnp.concatenate([first[:, 1:2], second[:, :2], second[:, 3:]], axis=1), "lat", 2, False
    )
    down = routed(
        jnp.concatenate([first[:, :2], second[:, :1], first[:, 2:3]], axis=1), "lat", -2, False
    )
    field = jnp.concatenate([up[:, :3], first[:, :2], second[:, :2], down[:, :3]], axis=1)
    grad = jnp.concatenate([up[:, 3:], first[:, 2:], second[:, 2:], down[:, 3:]], axis=1)
    lines = jnp.concatenate(
        [
            jnp.where(core == 0, field[:, :8], field[:, 2:]),
            jnp.where(core == 0, grad[:, :4], grad[:, 2:]),
        ],
        axis=1,
    )
    left = routed(lines[:, :, lond - EDGE :], "lon", 1, True)
    right = routed(lines[:, :, :EDGE], "lon", -1, True)
    return lines, left, right


def joined(left, lines, right):
    lond = lines.shape[2]
    blank = jnp.zeros(lines.shape[:2] + (WINDOW - lond - 2 * EDGE, lines.shape[3]), lines.dtype)
    return jnp.concatenate([left, lines, right, blank], axis=2)


def shards(inputs, cotangent, weights, psi, band_half):
    lat = lax.axis_index("lat")
    core = lat % 2
    segment = lax.axis_index("segment")
    matrix = weights[0]
    half = matrix.shape[0] // 2
    mine = lax.dynamic_slice_in_dim(matrix, core * half, half, 0)
    other_near = lax.ppermute(mine, ("segment", "lon"), across())
    lines, left, right = widened(inputs, cotangent)
    tables = band_tables(*tap_rows(psi, band_half, lat * inputs.shape[1]))
    left, right, other_near, tables = lax.optimization_barrier((left, right, other_near, tables))
    other_far = lax.ppermute(
        other_near, "lat", [(i, i ^ 1) for i in range(lax.axis_size("lat"))]
    )
    field = joined(left, lines, right)
    flags = jnp.stack([segment, core]).astype(jnp.int32)
    section, keep, give = on_device(
        flags, tables, field, matrix, other_near, other_far, inputs.shape[2]
    )
    return (section[None], gathered_sum(keep, give)[None])


def solution(mesh):
    placed = (
        P(None, "lat", "lon", None),
        P(None, "lat", "lon", None),
        P("segment", None, None),
        P(),
        P(),
    )
    return jax.shard_map(
        shards,
        mesh=mesh,
        in_specs=placed,
        out_specs=(P("segment", None, "lat", "lon", None), P("segment", None, None)),
        check_vma=False,
    )
```

```python
import functools

import jax
import jax.numpy as jnp
from jax import lax
from jax.experimental import pallas as pl
from jax.experimental.pallas import tpu as pltpu
from jax.sharding import PartitionSpec as P

EDGE = 24
WINDOW = 112
FIRST = 80
SECOND = 64
BLOCK = 48
REST = 32
SLAB = 64
WIDE = 256
DEEP = 640
CURVE = 0.7978845608028654
CUBIC = 0.044715


def routed(block, axis, distance, closed):
    count = lax.axis_size(axis)
    if closed:
        route = [(i, (i + distance) % count) for i in range(count)]
    else:
        route = [(i, i + distance) for i in range(count) if 0 <= i + distance < count]
    return lax.ppermute(block, axis, route)


def gelu_slope(x):
    squared = x * x
    bend = jnp.tanh(CURVE * (x + CUBIC * x * squared))
    inner = CURVE * (1.0 + 3.0 * CUBIC * squared)
    return 0.5 * (1.0 + bend) + 0.5 * x * (1.0 - bend * bend) * inner


def table_kernel(ahead, behind, table, adjoint):
    kernels = ahead.shape[1]
    bf16 = jnp.bfloat16

    def sloped(row, lines, start):
        return pltpu.roll(
            jnp.broadcast_to(row, (lines, 128)), start, 1, stride=1, stride_axis=0
        )

    def forward(r, carry):
        for k in range(kernels):
            for part in (slice(0, 128), slice(128, 256)):
                table[r * kernels + k, :, part] = sloped(
                    ahead[r, k : k + 1, part], BLOCK, 0
                ).astype(bf16)
        return carry

    lax.fori_loop(0, ahead.shape[0], forward, 0)
    low = lax.broadcasted_iota(jnp.int32, (FIRST, 128), 1) < SECOND

    def backward(i, carry):
        for pair in range(DEEP // 128):
            k = 2 * pair
            even = sloped(behind[i, k : k + 1, :], FIRST, SECOND)
            if k + 1 < kernels:
                odd = sloped(behind[i, k + 1 : k + 2, :], FIRST, 0)
            else:
                odd = jnp.zeros_like(even)
            adjoint[i, :, pair * 128 : (pair + 1) * 128] = jnp.where(low, even, odd).astype(bf16)
        return carry

    lax.fori_loop(0, behind.shape[0], backward, 0)


def band_tables(ahead, behind):
    whole = pl.BlockSpec(memory_space=pltpu.VMEM)
    lines, kernels = ahead.shape[:2]
    return pl.pallas_call(
        table_kernel,
        out_shape=(
            jax.ShapeDtypeStruct((lines * kernels, BLOCK, WIDE), jnp.bfloat16),
            jax.ShapeDtypeStruct((behind.shape[0], FIRST, DEEP), jnp.bfloat16),
        ),
        in_specs=[whole] * 2,
        out_specs=(whole, whole),
        compiler_params=pltpu.CompilerParams(vmem_limit_bytes=16 * 1024 * 1024),
        name="tables",
    )(ahead, behind)


def device_kernel(
    flags,
    table,
    adjoint,
    field,
    own_matrix,
    other_near,
    other_far,
    section,
    keep,
    give,
    matrices,
    turned,
    basis0,
    basis1,
    middle,
    preact0,
    units1,
    spread,
    chosen_basis,
    chosen_units,
    grads,
):
    f32, bf16 = jnp.float32, jnp.bfloat16
    rows, chans = own_matrix.shape
    kernels = rows // chans
    half = rows // 2
    segment, core = flags[0], flags[1]
    lond = section.shape[2]
    near_start = pl.multiple_of(core * half, half)
    far_start = pl.multiple_of((1 - core) * half, half)

    def convolve(m, r, line, source, basis, start, pieces):
        for offset, count in pieces:
            blocks = [source[m, r + min(a, 2), offset : offset + SLAB] for a in range(4)]
            slab = jnp.concatenate(blocks, axis=0)
            rows_of = table[pl.ds(line * kernels, kernels), :count].reshape(kernels * count, WIDE)
            out = jnp.dot(rows_of, slab, preferred_element_type=f32)
            place = pl.multiple_of(start + offset, 16)
            for k in range(kernels):
                basis[pl.ds(place, count), k * chans : (k + 1) * chans] = out[
                    k * count : (k + 1) * count
                ].astype(bf16)

    def first_basis(r, carry):
        for m in range(2):
            convolve(m, r, r, field, basis0, (m * 6 + r) * FIRST, ((0, BLOCK), (BLOCK, REST)))
        return carry

    lax.fori_loop(0, 6, first_basis, 0, unroll=True)

    matrices[segment] = own_matrix[...]
    matrices[1 - segment, pl.ds(near_start, half)] = other_near[...]
    matrices[1 - segment, pl.ds(far_start, half)] = other_far[...]

    for k in range(kernels):
        span = slice(k * chans, (k + 1) * chans)
        turned[:, span] = jnp.transpose(matrices[1, span, :])

    def first_mix(m, carry):
        start = pl.multiple_of(m * 6 * FIRST, 16)
        pre = jnp.dot(
            basis0[pl.ds(start, 6 * FIRST), :], matrices[0], preferred_element_type=f32
        )
        centre = field[m, 1:7].astype(f32)[:, 8 : 8 + FIRST].reshape(6 * FIRST, chans)
        out = centre + jax.nn.gelu(pre)
        middle[m, :, :FIRST] = out.astype(bf16).reshape(6, FIRST, chans)
        middle[m, :, FIRST:] = jnp.zeros((6, 16, chans), bf16)
        for p in range(2):
            preact0[m, p] = pre[(p + 2) * FIRST + 16 : (p + 3) * FIRST]
        return carry

    lax.fori_loop(0, 2, first_mix, 0, unroll=True)

    def second_basis(s, carry):
        for m in range(2):
            start = (m * 4 + s) * SECOND
            convolve(m, s, s + 1, middle, basis1, start, ((0, REST), (REST, REST)))
        return carry

    lax.fori_loop(0, 4, second_basis, 0, unroll=True)

    def second_mix(m, carry):
        start = pl.multiple_of(m * 4 * SECOND, 4 * SECOND)
        pre = jnp.dot(
            basis1[pl.ds(start, 4 * SECOND), :], matrices[1], preferred_element_type=f32
        )
        incoming = field[m, 8:12, 16 : 16 + SECOND].astype(f32).reshape(4 * SECOND, chans)
        units1[pl.ds(start, 4 * SECOND), :] = (incoming * gelu_slope(pre)).astype(bf16)
        for p in range(2):
            own = middle[m, p + 2, 16 : 16 + SECOND].astype(f32)[:lond]
            begin = (p + 1) * SECOND + 8
            late = own + jax.nn.gelu(pre[begin : begin + lond])
            section[m, p] = jnp.where(segment == 0, own, late).astype(bf16)
        return carry

    lax.fori_loop(0, 2, second_mix, 0, unroll=True)

    column = lax.broadcasted_iota(jnp.int32, (SECOND, chans), 0)

    @pl.when(segment == 0)
    def _():
        live = column < lond
        spread[:, kernels * SECOND :, :] = jnp.zeros(
            (4, DEEP - kernels * SECOND, 2 * chans), bf16
        )
        for k in range(kernels):
            mixed = lax.dot_general(
                units1[...],
                turned[:, k * chans : (k + 1) * chans],
                (((1,), (0,)), ((), ())),
                preferred_element_type=f32,
            ).astype(bf16)
            for m in range(2):
                for s in range(4):
                    begin = (m * 4 + s) * SECOND
                    spread[
                        s, k * SECOND : (k + 1) * SECOND, m * chans : (m + 1) * chans
                    ] = mixed[begin : begin + SECOND]
        for p in range(2):
            back = jnp.zeros((FIRST, 2 * chans), f32)
            for a in range(3):
                s = p + 2 - a
                back += jnp.dot(adjoint[s * 3 + a], spread[s], preferred_element_type=f32)
            for m in range(2):
                place = (m * 2 + p) * SECOND
                total = field[m, 9 + p].astype(f32)[EDGE : EDGE + SECOND] + back[
                    16 : 16 + SECOND, m * chans : (m + 1) * chans
                ]
                grad = total.astype(bf16).astype(f32)
                unit = grad * gelu_slope(preact0[m, p])
                chosen_units[place : place + SECOND, :] = jnp.where(live, unit, 0.0).astype(bf16)
                begin = (m * 6 + p + 2) * FIRST + 16
                chosen_basis[place : place + SECOND, :] = basis0[begin : begin + SECOND, :]

    @pl.when(segment != 0)
    def _():
        live = (column >= 8) & (column < 8 + lond)
        for p in range(2):
            for m in range(2):
                place = (m * 2 + p) * SECOND
                begin = (m * 4 + p + 1) * SECOND
                unit = units1[begin : begin + SECOND, :].astype(f32)
                chosen_units[place : place + SECOND, :] = jnp.where(live, unit, 0.0).astype(bf16)
                chosen_basis[place : place + SECOND, :] = basis1[begin : begin + SECOND, :]

    for k in range(kernels):
        grads[k * chans : (k + 1) * chans, :] = lax.dot_general(
            chosen_basis[:, k * chans : (k + 1) * chans],
            chosen_units[...],
            (((0,), (0,)), ((), ())),
            preferred_element_type=f32,
        )
    keep[...] = grads[pl.ds(near_start, half), :]
    give[...] = grads[pl.ds(far_start, half), :].astype(bf16)


def on_device(flags, tables, field, own_matrix, other_near, other_far, lond):
    rows, chans = own_matrix.shape
    half = rows // 2
    bf16, f32 = jnp.bfloat16, jnp.float32
    whole = pl.BlockSpec(memory_space=pltpu.VMEM)
    return pl.pallas_call(
        device_kernel,
        out_shape=(
            jax.ShapeDtypeStruct((2, 2, lond, chans), bf16),
            jax.ShapeDtypeStruct((half, chans), f32),
            jax.ShapeDtypeStruct((half, chans), bf16),
        ),
        in_specs=[pl.BlockSpec(memory_space=pltpu.SMEM)] + [whole] * 6,
        out_specs=(whole, whole, whole),
        scratch_shapes=[
            pltpu.VMEM((2, rows, chans), bf16),
            pltpu.VMEM((chans, rows), bf16),
            pltpu.VMEM((12 * FIRST, rows), bf16),
            pltpu.VMEM((8 * SECOND, rows), bf16),
            pltpu.VMEM((2, 6, FIRST + 16, chans), bf16),
            pltpu.VMEM((2, 2, SECOND, chans), f32),
            pltpu.VMEM((8 * SECOND, chans), bf16),
            pltpu.VMEM((4, DEEP, 2 * chans), bf16),
            pltpu.VMEM((4 * SECOND, rows), bf16),
            pltpu.VMEM((4 * SECOND, chans), bf16),
            pltpu.VMEM((rows, chans), f32),
        ],
        compiler_params=pltpu.CompilerParams(vmem_limit_bytes=32 * 1024 * 1024),
        name="sphere",
    )(flags, *tables, field, own_matrix, other_near, other_far)


def gathered_sum(keep, give):
    lats, lons = lax.axis_size("lat"), lax.axis_size("lon")
    half, chans = keep.shape
    depth = 16
    planes = lons // depth
    columns = lats // 2 * planes
    swap = [(i, i ^ 1) for i in range(lats)]
    near = [
        [(2 * y + core) * lons + x * depth + z for y in range(lats // 2) for x in range(planes)]
        for core in range(2)
        for z in range(depth)
    ]
    hop = 4
    beside = [[b + i for i in range(hop)] for b in range(0, lons, hop)]
    apart = [
        [x * depth + b + i * hop for i in range(depth // hop)]
        for x in range(planes)
        for b in range(hop)
    ]
    core = lax.axis_index("lat") % 2
    own = (keep + lax.ppermute(give, "lat", swap).astype(jnp.float32)).astype(jnp.bfloat16)
    own = own.reshape(columns, half // columns, chans)
    own = lax.all_to_all(own, ("lat", "lon"), 0, 0, axis_index_groups=near)
    own = jnp.sum(own.astype(jnp.float32), axis=0).astype(jnp.bfloat16)
    lines, lanes = half // columns // 2, chans // 2
    own = own.reshape(2, lines, 2, lanes).transpose(0, 2, 1, 3).reshape(hop, lines, lanes)
    own = lax.all_to_all(own, "lon", 0, 0, axis_index_groups=beside)
    own = jnp.sum(own.astype(jnp.float32), axis=0).astype(jnp.bfloat16)
    own = jnp.broadcast_to(own[None], (depth // hop,) + own.shape)
    own = lax.all_to_all(own, "lon", 0, 0, axis_index_groups=apart)
    own = jnp.sum(own.astype(jnp.float32), axis=0).astype(jnp.bfloat16)
    own = jnp.broadcast_to(own[None], (hop,) + own.shape)
    own = lax.all_to_all(own, "lon", 0, 0, axis_index_groups=beside)
    own = own.reshape(2, 2, lines, lanes).transpose(0, 2, 1, 3).reshape(2 * lines, chans)
    own = jnp.broadcast_to(own[None], (columns,) + own.shape)
    own = lax.all_to_all(own, ("lat", "lon"), 0, 0, axis_index_groups=near).reshape(-1, chans)
    other = lax.ppermute(own, "lat", swap)
    whole = jnp.zeros((2 * half, chans), jnp.float32)
    whole = lax.dynamic_update_slice_in_dim(whole, own.astype(jnp.float32), core * half, 0)
    return lax.dynamic_update_slice_in_dim(
        whole, other.astype(jnp.float32), (1 - core) * half, 0
    )


def tap_rows(psi, band_half, lat_start):
    kernels, lines, offsets, width = psi.shape
    taps = lax.broadcasted_iota(jnp.int32, psi.shape, 3)
    live = jnp.abs(taps - (width - 1) // 2) <= band_half[None, :, :, None]
    effective = jnp.where(live, psi, jnp.zeros_like(psi)).astype(jnp.float32)
    by_row = jnp.transpose(effective, (1, 0, 2, 3))
    by_row = jnp.pad(by_row, ((2, 2), (0, 0), (0, 0), (0, 0)))
    own = lax.dynamic_slice_in_dim(by_row, lat_start, 6, 0)
    ahead = jnp.pad(own, ((0, 0), (0, 0), (0, 1), (0, SLAB - width)))
    ahead = ahead.reshape(6, kernels, WIDE)
    behind = jnp.transpose(jnp.flip(own[1:5], 3), (0, 2, 1, 3))
    start = SECOND - width + 1
    behind = jnp.pad(behind, ((0, 0), (0, 0), (0, 0), (start, 128 - width - start)))
    return ahead, behind.reshape(4 * offsets, kernels, 128)


def across():
    lons = lax.axis_size("lon")
    depth = lons // 2
    return [
        (seg * lons + x * depth + z, (1 - seg) * lons + (1 - x) * depth + z)
        for seg in range(2)
        for x in range(2)
        for z in range(depth)
    ]


def widened(inputs, cotangent):
    lond = inputs.shape[2]
    lats = lax.axis_size("lat")
    core = lax.axis_index("lat") % 2
    own = jnp.concatenate([inputs, cotangent], axis=1)
    mate = lax.ppermute(own, "lat", [(i, i ^ 1) for i in range(lats)])
    first = jnp.where(core == 0, own, mate)
    second = jnp.where(core == 0, mate, own)
    up = routed(
        jnp.concatenate([first[:, 1:2], second[:, :2], second[:, 3:]], axis=1), "lat", 2, False
    )
    down = routed(
        jnp.concatenate([first[:, :2], second[:, :1], first[:, 2:3]], axis=1), "lat", -2, False
    )
    field = jnp.concatenate([up[:, :3], first[:, :2], second[:, :2], down[:, :3]], axis=1)
    grad = jnp.concatenate([up[:, 3:], first[:, 2:], second[:, 2:], down[:, 3:]], axis=1)
    lines = jnp.concatenate(
        [
            jnp.where(core == 0, field[:, :8], field[:, 2:]),
            jnp.where(core == 0, grad[:, :4], grad[:, 2:]),
        ],
        axis=1,
    )
    right = routed(lines[:, :, :EDGE], "lon", -1, True)
    left = routed(lines[:, :, lond - EDGE :], "lon", 1, True)
    return lines, left, right


def joined(left, lines, right):
    lond = lines.shape[2]
    blank = jnp.zeros(lines.shape[:2] + (WINDOW - lond - 2 * EDGE, lines.shape[3]), lines.dtype)
    return jnp.concatenate([left, lines, right, blank], axis=2)


def shards(inputs, cotangent, weights, psi, band_half):
    lat = lax.axis_index("lat")
    core = lat % 2
    segment = lax.axis_index("segment")
    matrix = weights[0]
    half = matrix.shape[0] // 2
    mine = lax.dynamic_slice_in_dim(matrix, core * half, half, 0)
    other_near = lax.ppermute(mine, ("segment", "lon"), across())
    lines, left, right = widened(inputs, cotangent)
    tables = band_tables(*tap_rows(psi, band_half, lat * inputs.shape[1]))
    left, right, other_near, tables = lax.optimization_barrier((left, right, other_near, tables))
    other_far = lax.ppermute(
        other_near, "lat", [(i, i ^ 1) for i in range(lax.axis_size("lat"))]
    )
    field = joined(left, lines, right)
    flags = jnp.stack([segment, core]).astype(jnp.int32)
    section, keep, give = on_device(
        flags, tables, field, matrix, other_near, other_far, inputs.shape[2]
    )
    return (section[None], gathered_sum(keep, give)[None])


def solution(mesh):
    placed = (
        P(None, "lat", "lon", None),
        P(None, "lat", "lon", None),
        P("segment", None, None),
        P(),
        P(),
    )
    return jax.shard_map(
        shards,
        mesh=mesh,
        in_specs=placed,
        out_specs=(P("segment", None, "lat", "lon", None), P("segment", None, None)),
        check_vma=False,
    )
```
